32 devices in a mesh: row: 4 (over z), col: 8 (over y, x, core).
Axes of the slice: x: 2, y: 2, z: 4, core: 2. Of those that a mesh axis runs over, the one named last changes fastest.
Arguments:
- operator_tiles: bfloat16 [16, 32, 9, 64, 64], P('row', 'col'), may hold values from -0.25 to 0.25
- neighbour_codes: int32 [16, 32, 9], P('row', 'col'), may hold values from 0 to 8, as said below
- live_slots: int32 [16, 32], P('row', 'col'), may hold values from 1 to 9, as said below
- prolong_tiles: bfloat16 [16, 32, 6, 64, 64], P('row', 'col'), may hold values from -0.75 to 0.75
- coarse_blocks: int32 [16, 32, 6], P('row', 'col'), may hold values from 0 to 31, as said below
Outputs:
- coarse_band: float32 [8, 256, 1792], P('col', 'row')
The draws below stay inside these ranges and needn't reach their ends.
Inputs may be any that keep to these rules, and one draw needn't show every extreme that they name: `neighbour_codes`: A fine block's 9 codes differ; slot 0 holds 4, the block itself. Slots 0 to live_slots - 1 of a fine block are used; some fine block uses all 9. `coarse_blocks`: the 6 coarse blocks of a fine block in slab s differ and lie in slabs s - 1, s, s + 1 (mod 8); the first lies in slab s.
All inputs are finite; a program needn't handle non-finite values.
Results may differ from the reference program's by a relative error of at most 0.0029.
Values may be sent and summed in bfloat16 or wider, within the bound.
A program may use at most 128 MiB of HBM per device.

```python
import jax
import jax.numpy as jnp
from jax import lax

BLK = 64
KA = 9
KP = 6
CB = 4
FX = 4
FY = 4
NXB = 16
NYB = 32
N_ROW = 4
N_COL = 8


def draw_neighbour_codes(key, part):
    first_count = N_ROW * FX
    second_count = N_COL * FY
    codes = jnp.arange(9, dtype=jnp.int32)
    scores = jax.random.randint(jax.random.fold_in(key, 5), (first_count, second_count, 9), 0, 1 << 20) * 16 + codes
    scores = jnp.where(codes == 4, -1, scores)
    ordered = jnp.argsort(scores, axis=-1)
    return ordered[..., :KA].astype(jnp.int32)


def draw_live_slots(key, part):
    first_count = N_ROW * FX
    second_count = N_COL * FY
    keys = jax.random.split(jax.random.fold_in(key, 11), 3)
    density = jax.random.randint(keys[0], (N_ROW, N_COL), 2, KA + 1)
    density = jnp.repeat(jnp.repeat(density, FX, axis=0), FY, axis=1)
    counts = 1 + jax.random.randint(keys[1], (first_count, second_count), 0, 1 << 20) % density
    chosen_spot = jax.random.randint(keys[2], (), 0, first_count * second_count)
    flat_index = jnp.arange(first_count * second_count).reshape(first_count, second_count)
    return jnp.where(flat_index == chosen_spot, KA, counts).astype(jnp.int32)


def draw_coarse_blocks(key, part):
    first_count = N_ROW * FX
    second_count = N_COL * FY
    keys = jax.random.split(jax.random.fold_in(key, 23), 2)
    aggregate = jax.random.randint(keys[0], (first_count, second_count), 0, CB)
    codes = jnp.arange(3 * CB, dtype=jnp.int32)
    scores = jax.random.randint(keys[1], (first_count, second_count, 3 * CB), 0, 1 << 18) * 4096 + codes
    scores = jnp.where(codes == CB + aggregate[..., None], -1, scores)
    chosen = jnp.argsort(scores, axis=-1)[..., :KP]
    slab_number = (jnp.arange(second_count) // FY)[None, :, None]
    return (jnp.mod(slab_number + chosen // CB - 1, N_COL) * CB + chosen % CB).astype(jnp.int32)


def block_scale(stream_key, shape, cuts, low, largest):
    loudness, own = 1.0, jax.random.fold_in(stream_key, 6)
    for dim, parts in cuts:
        heights = jnp.exp(jax.random.uniform(jax.random.fold_in(own, dim), (parts,), jnp.float32, low / len(cuts), largest / len(cuts)))
        loudness = loudness * jnp.repeat(heights, shape[dim] // parts).reshape([-1 if axis == dim else 1 for axis in range(len(shape))])
    return loudness


def normal_values(rng, extent, scale, bound, shards=(), held_as=jnp.bfloat16):
    gain = block_scale(rng, extent, shards, -0.22, 0.18) if shards else 1.0
    values = jax.random.normal(rng, extent, jnp.float32) * scale * gain
    return jnp.minimum(jnp.maximum(values, -bound), bound).astype(held_as)


def setup_inputs(seed: int = 0) -> dict:
    seeds = jax.random.split(jax.random.key(seed), 6)
    operator_tiles = normal_values(seeds[0], (NXB, NYB, KA, BLK, BLK), (KA * BLK) ** -0.5, 0.25, ((0, 4), (1, 8)))
    neighbour_codes = draw_neighbour_codes(jax.random.fold_in(seeds[5], 71), 0)
    live_slots = draw_live_slots(jax.random.fold_in(seeds[5], 71), 0)
    prolong_tiles = normal_values(seeds[3], (NXB, NYB, KP, BLK, BLK), BLK ** -0.5, 0.75, ((0, 4), (1, 8)))
    coarse_blocks = draw_coarse_blocks(jax.random.fold_in(seeds[5], 71), 0)
    return {"operator_tiles": operator_tiles, "neighbour_codes": neighbour_codes, "live_slots": live_slots, "prolong_tiles": prolong_tiles, "coarse_blocks": coarse_blocks}


def reference(operator_tiles, neighbour_codes, live_slots, prolong_tiles, coarse_blocks):
    highest = lax.Precision.HIGHEST
    window_cols = 5 * CB
    window_rows = 3 * CB
    zero_index = jnp.zeros((), jnp.int32)

    def slab_partial(slab_index):
        col_start = (slab_index * FY).astype(jnp.int32)
        second_index = col_start + jnp.arange(FY, dtype=jnp.int32)

        def row_step(running, row_block):
            op_row = lax.dynamic_slice(operator_tiles, (row_block, col_start, zero_index, zero_index, zero_index), (1, FY, KA, BLK, BLK))[0]
            codes_row = lax.dynamic_slice(neighbour_codes, (row_block, col_start, zero_index), (1, FY, KA))[0]
            live_row = lax.dynamic_slice(live_slots, (row_block, col_start), (1, FY))[0]
            own_tiles = lax.dynamic_slice(prolong_tiles, (row_block, col_start, zero_index, zero_index, zero_index), (1, FY, KP, BLK, BLK))[0]
            own_blocks = lax.dynamic_slice(coarse_blocks, (row_block, col_start, zero_index), (1, FY, KP))[0]
            near_first = jnp.mod(row_block + codes_row // 3 - 1, NXB).astype(jnp.int32)
            near_second = jnp.mod(second_index[:, None] + codes_row % 3 - 1, NYB).astype(jnp.int32)
            near_tiles = prolong_tiles[near_first, near_second].astype(jnp.float32)
            near_blocks = coarse_blocks[near_first, near_second]
            col_place = jnp.mod(near_blocks // CB - slab_index + 2, N_COL) * CB + near_blocks % CB
            col_hot = (col_place[..., None] == jnp.arange(window_cols)).astype(jnp.float32)
            live_mask = (jnp.arange(KA) < live_row[:, None]).astype(jnp.float32)
            products = jnp.einsum("mkab,mklbc->mklac", op_row.astype(jnp.float32), near_tiles, precision=highest)
            products = products * live_mask[:, :, None, None, None]
            image_panel = jnp.einsum("mklac,mklq->maqc", products, col_hot, precision=highest)
            image_panel = image_panel.reshape(FY, BLK, window_cols * BLK).astype(jnp.bfloat16)
            row_place = jnp.mod(own_blocks // CB - slab_index + 1, N_COL) * CB + own_blocks % CB
            row_hot = (row_place[..., None] == jnp.arange(window_rows)).astype(jnp.float32)
            contrib = jnp.einsum("mlba,mbc->mlac", own_tiles.astype(jnp.float32), image_panel.astype(jnp.float32), precision=highest)
            running = running + jnp.einsum("mlac,mlr->rac", contrib, row_hot, precision=highest)
            return running, None

        start_sum = jnp.zeros((window_rows, BLK, window_cols * BLK), jnp.float32)
        total, unused = lax.scan(row_step, start_sum, jnp.arange(NXB, dtype=jnp.int32))
        return total.reshape(3, CB * BLK, window_cols * BLK)

    partials = lax.map(slab_partial, jnp.arange(N_COL, dtype=jnp.int32))
    slab_rows = CB * BLK
    own_rows = partials[:, 1]
    from_next = jnp.roll(partials[:, 0], -1, axis=0)
    from_prev = jnp.roll(partials[:, 2], 1, axis=0)
    combined = jnp.pad(own_rows, ((0, 0), (0, 0), (slab_rows, slab_rows)))
    combined = combined + jnp.pad(from_next, ((0, 0), (0, 0), (2 * slab_rows, 0)))
    combined = combined + jnp.pad(from_prev, ((0, 0), (0, 0), (0, 2 * slab_rows)))
    return combined
```

```python
import functools

import jax
import jax.numpy as jnp
from jax import lax
from jax.experimental import pallas as pl
from jax.experimental.pallas import tpu as pltpu
from jax.sharding import PartitionSpec as P

CB = 4
MESH = pl.DeviceIdType.MESH
STRIDE = 16


def kernel(
    dims, n_row, n_col, a_ref, p_ref, ainv_ref, codes_smem, codes_ref, out_ref,
    pext, cext, csm, p2, wc, wl, wr, wt, ac, al, ar, acc, img,
    csend, crecv, own, zsend, zrecv,
    psend_sem, precv_sem, ksend_sem, krecv_sem, copy_sem,
    csend_sem, crecv_sem, zsend_sem, zrecv_sem,
):
    fx, fy, ka, kp, b = dims
    win = 3 * CB
    slab = CB * b
    rows = slab // n_row
    wide = 5 * slab
    me_r, me_c = lax.axis_index("row"), lax.axis_index("col")

    def device(dr, dc):
        return (lax.rem(me_r + dr + n_row, n_row), lax.rem(me_c + dc + n_col, n_col))

    around = [(i, j) for i in (-1, 0, 1) for j in (-1, 0, 1) if (i, j) != (0, 0)]
    partners = {(i % n_row, j % n_col) for i, j in around} | {(k, 0) for k in range(1, n_row)}
    barrier = pltpu.get_barrier_semaphore()
    for i, j in sorted(partners):
        pl.semaphore_signal(barrier, inc=1, device_id=device(i, j), device_id_type=MESH)

    def pack(n, carry):
        x, y = n // fy, n % fy
        for j in range(0, kp, 2):
            pair = [p_ref[n * kp + j], p_ref[n * kp + j + 1]]
            pext[x + 1, y + 1, :, j * b:(j + 2) * b] = jnp.concatenate(pair, axis=1)
        return carry

    lax.fori_loop(0, fx * fy, pack, 0)
    pl.semaphore_wait(barrier, len(partners))

    halo = []
    for t, (i, j) in enumerate(around):
        xs = {-1: 1, 0: pl.ds(1, fx), 1: fx}[i]
        ys = {-1: 1, 0: pl.ds(1, fy), 1: fy}[j]
        xd = {-1: fx + 1, 0: pl.ds(1, fx), 1: 0}[i]
        yd = {-1: fy + 1, 0: pl.ds(1, fy), 1: 0}[j]
        numbers = pltpu.make_async_remote_copy(
            src_ref=codes_ref, dst_ref=cext.at[(1 - i) * 3 + 1 - j],
            send_sem=ksend_sem.at[t], recv_sem=krecv_sem.at[t],
            device_id=device(i, j), device_id_type=MESH,
        )
        tiles = pltpu.make_async_remote_copy(
            src_ref=pext.at[xs, ys], dst_ref=pext.at[xd, yd],
            send_sem=psend_sem.at[t], recv_sem=precv_sem.at[t],
            device_id=device(i, j), device_id_type=MESH,
        )
        halo += [numbers, tiles]
    for copy in halo:
        copy.start()

    lane = lax.broadcasted_iota(jnp.int32, (b, 2 * b), 1)
    lower = lane < b

    def spread(xe, ye, n, read, dst, at):
        e = xe * (fy + 2) + ye
        p2[e, kp] = jnp.zeros((b, 2 * b), p2.dtype)
        for j in range(0, kp, 2):
            pair = pext[xe, ye, :, j * b:(j + 2) * b]
            for h in range(2):
                tile = pair[:, h * b:(h + 1) * b]
                p2[e, j + h] = jnp.concatenate([tile, tile], axis=1)
        for w in range(0, win, 2):
            flat = n * STRIDE + w
            first, second = read(flat), read(flat + 1)
            dst(at, w * b, jnp.where(lower, p2[e, first], p2[e, second]))

    def to_centre(at, c, value):
        wc[at[0], pl.ds(at[1], b), c:c + 2 * b] = value

    def to_left(at, c, value):
        wl[pl.ds(at, b), c:c + 2 * b] = value

    def to_right(at, c, value):
        wr[pl.ds(at, b), c:c + 2 * b] = value

    def read_own(flat):
        return codes_smem[flat // 128, flat % 128]

    def read_near(slot):
        return lambda flat: csm[slot, flat // 128, flat % 128]

    def own_spread(n, carry):
        x, y = n // fy, n % fy
        spread(x + 1, y + 1, n, read_own, to_centre, (x + 1, pl.multiple_of(y * b, b)))
        return carry

    lax.fori_loop(0, fx * fy, own_spread, 0)

    def operator_tile(m, d):
        k = ainv_ref[m * 9 + d]
        tile = a_ref[m * ka + jnp.minimum(k, ka - 1)]
        return jnp.where(jnp.full(tile.shape, k) < ka, tile, jnp.zeros_like(tile))

    zero_tile = jnp.zeros((b, b), a_ref.dtype)

    def bands(x, carry):
        for dx in range(3):
            for y in range(fy):
                for yp in range(0, fy, 2):
                    pair = [
                        operator_tile(x * fy + y, dx * 3 + yy - y + 1) if abs(yy - y) < 2 else zero_tile
                        for yy in (yp, yp + 1)
                    ]
                    ac[x * 3 + dx, y * b:(y + 1) * b, yp * b:(yp + 2) * b] = jnp.concatenate(pair, axis=1)
        return carry

    lax.fori_loop(0, fx, bands, 0)
    for x in range(fx):
        for side, y, dy in ((al, 0, 0), (ar, fy - 1, 2)):
            for xe in range(0, fx + 2, 2):
                pair = [
                    operator_tile(x * fy + y, (xx - x) * 3 + dy) if 0 <= xx - x <= 2 else zero_tile
                    for xx in (xe, xe + 1)
                ]
                side[x * b:(x + 1) * b, xe * b:(xe + 2) * b] = jnp.concatenate(pair, axis=1)

    def own_transposed(x, carry):
        for c in range(3):
            wt[c * slab:(c + 1) * slab, pl.ds(pl.multiple_of(x * fy * b, fy * b), fy * b)] = (
                wc[x + 1, :, c * slab:(c + 1) * slab].T
            )
        return carry

    lax.fori_loop(0, fx, own_transposed, 0)

    for x in range(fx):
        acc[x, :, 0:slab] = jnp.zeros((fy * b, slab), jnp.float32)
        acc[x, :, 4 * slab:] = jnp.zeros((fy * b, slab), jnp.float32)
        total = None
        for dx in range(3):
            if 1 <= x + dx <= fx:
                term = jnp.dot(ac[x * 3 + dx], wc[x + dx], preferred_element_type=jnp.float32)
                total = term if total is None else total + term
        acc[x, :, slab:4 * slab] = total

    for copy in halo:
        copy.wait_recv()
    numbers_in = pltpu.make_async_copy(cext, csm, copy_sem)
    numbers_in.start()
    numbers_in.wait()

    def edge_rows(y, carry):
        at = pl.multiple_of(y * b, b)
        spread(0, y + 1, (fx - 1) * fy + y, read_near(1), to_centre, (0, at))
        spread(fx + 1, y + 1, y, read_near(7), to_centre, (fx + 1, at))
        return carry

    lax.fori_loop(0, fy, edge_rows, 0)

    def edge_columns(x, carry):
        at = pl.multiple_of((x + 1) * b, b)
        spread(x + 1, 0, x * fy + fy - 1, read_near(3), to_left, at)
        spread(x + 1, fy + 1, x * fy, read_near(5), to_right, at)
        return carry

    lax.fori_loop(0, fx, edge_columns, 0)
    spread(0, 0, fx * fy - 1, read_near(0), to_left, 0)
    spread(0, fy + 1, (fx - 1) * fy, read_near(2), to_right, 0)
    spread(fx + 1, 0, fy - 1, read_near(6), to_left, (fx + 1) * b)
    spread(fx + 1, fy + 1, 0, read_near(8), to_right, (fx + 1) * b)

    acc[0, :, slab:4 * slab] += jnp.dot(ac[0], wc[0], preferred_element_type=jnp.float32)
    acc[fx - 1, :, slab:4 * slab] += jnp.dot(
        ac[(fx - 1) * 3 + 2], wc[fx + 1], preferred_element_type=jnp.float32
    )
    left = jnp.dot(al[...], wl[...], preferred_element_type=jnp.float32)
    for x in range(fx):
        acc[x, 0:b, 0:3 * slab] += left[x * b:(x + 1) * b]
    right = jnp.dot(ar[...], wr[...], preferred_element_type=jnp.float32)
    for x in range(fx):
        acc[x, (fy - 1) * b:, 2 * slab:] += right[x * b:(x + 1) * b]
    for x in range(fx):
        img[x * fy * b:(x + 1) * fy * b, :] = acc[x].astype(img.dtype)

    order = [*range(1, n_row), 0]
    across = []
    for side, part, step in ((0, 0, -1), (1, 2, 1)):
        for c in range(5):
            piece = jnp.dot(
                wt[part * slab:(part + 1) * slab, :], img[:, c * slab:(c + 1) * slab],
                preferred_element_type=jnp.float32,
            ).astype(csend.dtype)
            csend[side, :, c * slab:(c + 1) * slab] = piece
        for k in order:
            t = pl.multiple_of(lax.rem(me_r + k, n_row) * rows, rows)
            copy = pltpu.make_async_remote_copy(
                src_ref=csend.at[side, pl.ds(t, rows)], dst_ref=crecv.at[side, pl.ds(t, rows)],
                send_sem=csend_sem.at[side, k], recv_sem=crecv_sem.at[side, k],
                device_id=device(0, step), device_id_type=MESH,
            )
            copy.start()
            across.append((k, copy))
    for c in range(5):
        own[:, c * slab:(c + 1) * slab] = jnp.dot(
            wt[slab:2 * slab, :], img[:, c * slab:(c + 1) * slab], preferred_element_type=jnp.float32
        )

    def combined(t):
        mine = own[pl.ds(t, rows), :]
        from_next = crecv[0, pl.ds(t, rows), :].astype(jnp.float32)
        from_prev = crecv[1, pl.ds(t, rows), :].astype(jnp.float32)
        parts = []
        for c in range(7):
            terms = [
                value[:, (c - shift) * slab:(c - shift + 1) * slab]
                for value, shift in ((mine, 1), (from_next, 2), (from_prev, 0))
                if 0 <= c - shift < 5
            ]
            parts.append(functools.reduce(jnp.add, terms))
        return parts

    down = []
    for k in order:
        for other, copy in across:
            if other == k:
                copy.wait_recv()
        t = pl.multiple_of(lax.rem(me_r + k, n_row) * rows, rows)
        for c, value in enumerate(combined(t)):
            if k:
                zsend[k, :, c * slab:(c + 1) * slab] = value.astype(zsend.dtype)
            else:
                out_ref[:, c * slab:(c + 1) * slab] = value
        if k:
            copy = pltpu.make_async_remote_copy(
                src_ref=zsend.at[k], dst_ref=zrecv.at[k],
                send_sem=zsend_sem.at[k], recv_sem=zrecv_sem.at[k],
                device_id=device(k, 0), device_id_type=MESH,
            )
            copy.start()
            down.append((k, copy))
    for k, copy in down:
        copy.wait_recv()
        out_ref[...] += zrecv[k].astype(jnp.float32)
    for copy in halo:
        copy.wait_send()
    for _, copy in across + down:
        copy.wait_send()


def per_device(operator_tiles, neighbour_codes, live_slots, prolong_tiles, coarse_blocks):
    fx, fy, ka = neighbour_codes.shape
    kp = prolong_tiles.shape[2]
    b = operator_tiles.shape[-1]
    n_row, n_col = lax.axis_size("row"), lax.axis_size("col")
    slab_index = lax.axis_index("col")
    win = 3 * CB
    slab = CB * b
    rows = slab // n_row
    band = 7 * slab
    blocks = fx * fy
    slots = jnp.arange(ka, dtype=jnp.int32)[:, None]
    match = (neighbour_codes[..., None] == jnp.arange(9, dtype=jnp.int32)) & (slots < live_slots[..., None, None])
    ainv = jnp.min(jnp.where(match, slots, ka), axis=2).reshape(-1)
    place = jnp.mod(coarse_blocks // CB - slab_index + 1, n_col) * CB + coarse_blocks % CB
    tiles = jnp.arange(kp, dtype=jnp.int32)[:, None]
    hit = place[..., None] == jnp.arange(STRIDE, dtype=jnp.int32)
    pinv = jnp.min(jnp.where(hit, tiles, kp), axis=2).reshape(-1, 128)
    codes = jnp.pad(pinv, ((0, -pinv.shape[0] % 8), (0, 0)))
    bf, f32 = jnp.bfloat16, jnp.float32
    dma = pltpu.SemaphoreType.DMA
    vmem = pl.BlockSpec(memory_space=pltpu.VMEM)
    smem = pl.BlockSpec(memory_space=pltpu.SMEM)
    out = pl.pallas_call(
        functools.partial(kernel, (fx, fy, ka, kp, b), n_row, n_col),
        out_shape=jax.ShapeDtypeStruct((rows, band), f32),
        in_specs=[vmem, vmem, smem, smem, vmem],
        out_specs=vmem,
        scratch_shapes=[
            pltpu.VMEM((fx + 2, fy + 2, b, kp * b), bf),
            pltpu.VMEM((9, *codes.shape), jnp.int32),
            pltpu.SMEM((9, *codes.shape), jnp.int32),
            pltpu.VMEM(((fx + 2) * (fy + 2), kp + 1, b, 2 * b), bf),
            pltpu.VMEM((fx + 2, fy * b, win * b), bf),
            pltpu.VMEM(((fx + 2) * b, win * b), bf),
            pltpu.VMEM(((fx + 2) * b, win * b), bf),
            pltpu.VMEM((win * b, blocks * b), bf),
            pltpu.VMEM((fx * 3, fy * b, fy * b), bf),
            pltpu.VMEM((fx * b, (fx + 2) * b), bf),
            pltpu.VMEM((fx * b, (fx + 2) * b), bf),
            pltpu.VMEM((fx, fy * b, 5 * slab), f32),
            pltpu.VMEM((blocks * b, 5 * slab), bf),
            pltpu.VMEM((2, slab, 5 * slab), bf),
            pltpu.VMEM((2, slab, 5 * slab), bf),
            pltpu.VMEM((slab, 5 * slab), f32),
            pltpu.VMEM((n_row, rows, band), bf),
            pltpu.VMEM((n_row, rows, band), bf),
            dma((8,)), dma((8,)), dma((8,)), dma((8,)), dma,
            dma((2, n_row)), dma((2, n_row)), dma((n_row,)), dma((n_row,)),
        ],
        compiler_params=pltpu.CompilerParams(
            collective_id=0, has_side_effects=True, vmem_limit_bytes=50 * 1024 * 1024
        ),
    )(
        operator_tiles.reshape(-1, b, b), prolong_tiles.reshape(-1, b, b), ainv, codes, codes,
    )
    return out[None]


def solution(mesh):
    in_specs = (
        P("row", "col", None, None, None),
        P("row", "col", None),
        P("row", "col"),
        P("row", "col", None, None, None),
        P("row", "col", None),
    )
    out_specs = P("col", "row", None)
    return jax.shard_map(
        per_device, mesh=mesh, in_specs=in_specs, out_specs=out_specs, check_vma=False
    )
```

```python
import functools

import jax
import jax.numpy as jnp
from jax import lax
from jax.experimental import pallas as pl
from jax.experimental.pallas import tpu as pltpu
from jax.sharding import PartitionSpec as P

CB = 4
MESH = pl.DeviceIdType.MESH
STRIDE = 16


def kernel(
    dims, n_row, n_col, a_hbm, p_hbm, ainv_ref, codes_smem, codes_ref, out_ref,
    a_ref, p_ref, pext, cext, csm, p2, wc, wl, wr, wt, ac, al, ar, acc, img,
    csend, crecv, own, zsend, zrecv,
    psend_sem, precv_sem, ksend_sem, krecv_sem, copy_sem, a_sem, p_sem,
    csend_sem, crecv_sem, zsend_sem, zrecv_sem,
):
    fx, fy, ka, kp, b = dims
    win = 3 * CB
    slab = CB * b
    rows = slab // n_row
    wide = 5 * slab
    me_r, me_c = lax.axis_index("row"), lax.axis_index("col")

    tiles_in = pltpu.make_async_copy(p_hbm, p_ref, p_sem)
    tiles_in.start()
    operator_in = pltpu.make_async_copy(a_hbm, a_ref, a_sem)
    operator_in.start()

    def device(dr, dc):
        return (lax.rem(me_r + dr + n_row, n_row), lax.rem(me_c + dc + n_col, n_col))

    around = [(i, j) for i in (-1, 0, 1) for j in (-1, 0, 1) if (i, j) != (0, 0)]
    partners = {(i % n_row, j % n_col) for i, j in around} | {(k, 0) for k in range(1, n_row)}
    barrier = pltpu.get_barrier_semaphore()
    for i, j in sorted(partners):
        pl.semaphore_signal(barrier, inc=1, device_id=device(i, j), device_id_type=MESH)

    def pack(n, carry):
        x, y = n // fy, n % fy
        for j in range(0, kp, 2):
            pair = [p_ref[n * kp + j], p_ref[n * kp + j + 1]]
            pext[x + 1, y + 1, :, j * b:(j + 2) * b] = jnp.concatenate(pair, axis=1)
        return carry

    tiles_in.wait()
    lax.fori_loop(0, fx * fy, pack, 0)
    pl.semaphore_wait(barrier, len(partners))

    halo = []
    for t, (i, j) in enumerate(around):
        xs = {-1: 1, 0: pl.ds(1, fx), 1: fx}[i]
        ys = {-1: 1, 0: pl.ds(1, fy), 1: fy}[j]
        xd = {-1: fx + 1, 0: pl.ds(1, fx), 1: 0}[i]
        yd = {-1: fy + 1, 0: pl.ds(1, fy), 1: 0}[j]
        numbers = pltpu.make_async_remote_copy(
            src_ref=codes_ref, dst_ref=cext.at[(1 - i) * 3 + 1 - j],
            send_sem=ksend_sem.at[t], recv_sem=krecv_sem.at[t],
            device_id=device(i, j), device_id_type=MESH,
        )
        tiles = pltpu.make_async_remote_copy(
            src_ref=pext.at[xs, ys], dst_ref=pext.at[xd, yd],
            send_sem=psend_sem.at[t], recv_sem=precv_sem.at[t],
            device_id=device(i, j), device_id_type=MESH,
        )
        halo += [numbers, tiles]
    for copy in halo:
        copy.start()

    lane = lax.broadcasted_iota(jnp.int32, (b, 2 * b), 1)
    lower = lane < b

    def spread(xe, ye, n, read, dst, at):
        e = xe * (fy + 2) + ye
        p2[e, kp] = jnp.zeros((b, 2 * b), p2.dtype)
        for j in range(0, kp, 2):
            pair = pext[xe, ye, :, j * b:(j + 2) * b]
            for h in range(2):
                tile = pair[:, h * b:(h + 1) * b]
                p2[e, j + h] = jnp.concatenate([tile, tile], axis=1)
        for w in range(0, win, 2):
            flat = n * STRIDE + w
            first, second = read(flat), read(flat + 1)
            dst(at, w * b, jnp.where(lower, p2[e, first], p2[e, second]))

    def to_centre(at, c, value):
        wc[at[0], pl.ds(at[1], b), c:c + 2 * b] = value

    def to_left(at, c, value):
        wl[pl.ds(at, b), c:c + 2 * b] = value

    def to_right(at, c, value):
        wr[pl.ds(at, b), c:c + 2 * b] = value

    def read_own(flat):
        return codes_smem[flat // 128, flat % 128]

    def read_near(slot):
        return lambda flat: csm[slot, flat // 128, flat % 128]

    def own_spread(n, carry):
        x, y = n // fy, n % fy
        spread(x + 1, y + 1, n, read_own, to_centre, (x + 1, pl.multiple_of(y * b, b)))
        return carry

    lax.fori_loop(0, fx * fy, own_spread, 0)

    def operator_tile(m, d):
        k = ainv_ref[m * 9 + d]
        tile = a_ref[m * ka + jnp.minimum(k, ka - 1)]
        return jnp.where(jnp.full(tile.shape, k) < ka, tile, jnp.zeros_like(tile))

    zero_tile = jnp.zeros((b, b), a_ref.dtype)
    operator_in.wait()

    def bands(x, carry):
        for dx in range(3):
            for y in range(fy):
                for yp in range(0, fy, 2):
                    pair = [
                        operator_tile(x * fy + y, dx * 3 + yy - y + 1) if abs(yy - y) < 2 else zero_tile
                        for yy in (yp, yp + 1)
                    ]
                    ac[x * 3 + dx, y * b:(y + 1) * b, yp * b:(yp + 2) * b] = jnp.concatenate(pair, axis=1)
        return carry

    lax.fori_loop(0, fx, bands, 0)
    for x in range(fx):
        for side, y, dy in ((al, 0, 0), (ar, fy - 1, 2)):
            for xe in range(0, fx + 2, 2):
                pair = [
                    operator_tile(x * fy + y, (xx - x) * 3 + dy) if 0 <= xx - x <= 2 else zero_tile
                    for xx in (xe, xe + 1)
                ]
                side[x * b:(x + 1) * b, xe * b:(xe + 2) * b] = jnp.concatenate(pair, axis=1)

    def own_transposed(x, carry):
        for c in range(3):
            wt[c * slab:(c + 1) * slab, pl.ds(pl.multiple_of(x * fy * b, fy * b), fy * b)] = (
                wc[x + 1, :, c * slab:(c + 1) * slab].T
            )
        return carry

    lax.fori_loop(0, fx, own_transposed, 0)

    for x in range(fx):
        acc[x, :, 0:slab] = jnp.zeros((fy * b, slab), jnp.float32)
        acc[x, :, 4 * slab:] = jnp.zeros((fy * b, slab), jnp.float32)
        total = None
        for dx in range(3):
            if 1 <= x + dx <= fx:
                term = jnp.dot(ac[x * 3 + dx], wc[x + dx], preferred_element_type=jnp.float32)
                total = term if total is None else total + term
        acc[x, :, slab:4 * slab] = total

    for copy in halo:
        copy.wait_recv()
    numbers_in = pltpu.make_async_copy(cext, csm, copy_sem)
    numbers_in.start()
    numbers_in.wait()

    def edge_rows(y, carry):
        at = pl.multiple_of(y * b, b)
        spread(0, y + 1, (fx - 1) * fy + y, read_near(1), to_centre, (0, at))
        spread(fx + 1, y + 1, y, read_near(7), to_centre, (fx + 1, at))
        return carry

    lax.fori_loop(0, fy, edge_rows, 0)

    def edge_columns(x, carry):
        at = pl.multiple_of((x + 1) * b, b)
        spread(x + 1, 0, x * fy + fy - 1, read_near(3), to_left, at)
        spread(x + 1, fy + 1, x * fy, read_near(5), to_right, at)
        return carry

    lax.fori_loop(0, fx, edge_columns, 0)
    spread(0, 0, fx * fy - 1, read_near(0), to_left, 0)
    spread(0, fy + 1, (fx - 1) * fy, read_near(2), to_right, 0)
    spread(fx + 1, 0, fy - 1, read_near(6), to_left, (fx + 1) * b)
    spread(fx + 1, fy + 1, 0, read_near(8), to_right, (fx + 1) * b)

    acc[0, :, slab:4 * slab] += jnp.dot(ac[0], wc[0], preferred_element_type=jnp.float32)
    acc[fx - 1, :, slab:4 * slab] += jnp.dot(
        ac[(fx - 1) * 3 + 2], wc[fx + 1], preferred_element_type=jnp.float32
    )
    left = jnp.dot(al[...], wl[...], preferred_element_type=jnp.float32)
    for x in range(fx):
        acc[x, 0:b, 0:3 * slab] += left[x * b:(x + 1) * b]
    right = jnp.dot(ar[...], wr[...], preferred_element_type=jnp.float32)
    for x in range(fx):
        acc[x, (fy - 1) * b:, 2 * slab:] += right[x * b:(x + 1) * b]
    for x in range(fx):
        img[x * fy * b:(x + 1) * fy * b, :] = acc[x].astype(img.dtype)

    relayed = n_row == 4
    if relayed:
        far = jnp.where(2 * me_r < n_row, 3, 1)
        order = [2, far, n_row - far, 0]
    else:
        order = [*range(1, n_row), 0]
    across = []
    for side, part, step in ((0, 0, -1), (1, 2, 1)):
        for c in range(5):
            piece = jnp.dot(
                wt[part * slab:(part + 1) * slab, :], img[:, c * slab:(c + 1) * slab],
                preferred_element_type=jnp.float32,
            ).astype(csend.dtype)
            csend[side, :, c * slab:(c + 1) * slab] = piece
        for turn, k in enumerate(order):
            t = pl.multiple_of(lax.rem(me_r + k, n_row) * rows, rows)
            copy = pltpu.make_async_remote_copy(
                src_ref=csend.at[side, pl.ds(t, rows)], dst_ref=crecv.at[side, pl.ds(t, rows)],
                send_sem=csend_sem.at[side, turn], recv_sem=crecv_sem.at[side, turn],
                device_id=device(0, step), device_id_type=MESH,
            )
            copy.start()
            across.append((turn, copy))
    for c in range(5):
        own[:, c * slab:(c + 1) * slab] = jnp.dot(
            wt[slab:2 * slab, :], img[:, c * slab:(c + 1) * slab], preferred_element_type=jnp.float32
        )

    def combined(t):
        mine = own[pl.ds(t, rows), :]
        from_next = crecv[0, pl.ds(t, rows), :].astype(jnp.float32)
        from_prev = crecv[1, pl.ds(t, rows), :].astype(jnp.float32)
        parts = []
        for c in range(7):
            terms = [
                value[:, (c - shift) * slab:(c - shift + 1) * slab]
                for value, shift in ((mine, 1), (from_next, 2), (from_prev, 0))
                if 0 <= c - shift < 5
            ]
            parts.append(functools.reduce(jnp.add, terms))
        return parts

    inner = (me_r > 0) & (me_r < n_row - 1)
    down = []
    for turn, k in enumerate(order):
        last = turn == n_row - 2
        for other, copy in across:
            if other == turn:
                copy.wait_recv()
        t = pl.multiple_of(lax.rem(me_r + k, n_row) * rows, rows)
        if relayed and last:
            @pl.when(inner)
            def _():
                down[0].wait_recv()

        for c, value in enumerate(combined(t)):
            at = slice(c * slab, (c + 1) * slab)
            if turn == n_row - 1:
                out_ref[:, at] = value
                continue
            zsend[turn, :, at] = value.astype(zsend.dtype)
            if relayed and last:
                @pl.when(inner)
                def _(value=value, at=at):
                    zsend[turn, :, at] = (value + zrecv[2, :, at].astype(jnp.float32)).astype(zsend.dtype)
        if turn == n_row - 1:
            continue
        steps = k
        if relayed and turn == 0:
            steps = jnp.where(inner, 2, jnp.where(me_r == 0, 1, n_row - 1))
        copy = pltpu.make_async_remote_copy(
            src_ref=zsend.at[turn], dst_ref=zrecv.at[k],
            send_sem=zsend_sem.at[turn], recv_sem=zrecv_sem.at[k],
            device_id=device(steps, 0), device_id_type=MESH,
        )
        copy.start()
        down.append(copy)

    def take(k):
        out_ref[...] += zrecv[k].astype(jnp.float32)

    if relayed:
        for k, copy in enumerate(down):
            if k == 0:
                @pl.when(jnp.logical_not(inner))
                def _():
                    down[0].wait_recv()
                    take(2)
            else:
                copy.wait_recv()
                take(order[k])
    else:
        for turn, copy in enumerate(down):
            copy.wait_recv()
            take(order[turn])
    for copy in halo:
        copy.wait_send()
    for copy in [copy for _, copy in across] + down:
        copy.wait_send()


def per_device(operator_tiles, neighbour_codes, live_slots, prolong_tiles, coarse_blocks):
    fx, fy, ka = neighbour_codes.shape
    kp = prolong_tiles.shape[2]
    b = operator_tiles.shape[-1]
    n_row, n_col = lax.axis_size("row"), lax.axis_size("col")
    slab_index = lax.axis_index("col")
    win = 3 * CB
    slab = CB * b
    rows = slab // n_row
    band = 7 * slab
    blocks = fx * fy
    slots = jnp.arange(ka, dtype=jnp.int32)[:, None]
    match = (neighbour_codes[..., None] == jnp.arange(9, dtype=jnp.int32)) & (slots < live_slots[..., None, None])
    ainv = jnp.min(jnp.where(match, slots, ka), axis=2).reshape(-1)
    place = jnp.mod(coarse_blocks // CB - slab_index + 1, n_col) * CB + coarse_blocks % CB
    tiles = jnp.arange(kp, dtype=jnp.int32)[:, None]
    hit = place[..., None] == jnp.arange(STRIDE, dtype=jnp.int32)
    pinv = jnp.min(jnp.where(hit, tiles, kp), axis=2).reshape(-1, 128)
    codes = jnp.pad(pinv, ((0, -pinv.shape[0] % 8), (0, 0)))
    bf, f32 = jnp.bfloat16, jnp.float32
    dma = pltpu.SemaphoreType.DMA
    vmem = pl.BlockSpec(memory_space=pltpu.VMEM)
    hbm = pl.BlockSpec(memory_space=pltpu.HBM)
    smem = pl.BlockSpec(memory_space=pltpu.SMEM)
    out = pl.pallas_call(
        functools.partial(kernel, (fx, fy, ka, kp, b), n_row, n_col),
        out_shape=jax.ShapeDtypeStruct((rows, band), f32),
        in_specs=[hbm, hbm, smem, smem, vmem],
        out_specs=vmem,
        scratch_shapes=[
            pltpu.VMEM((blocks * ka, b, b), bf),
            pltpu.VMEM((blocks * kp, b, b), bf),
            pltpu.VMEM((fx + 2, fy + 2, b, kp * b), bf),
            pltpu.VMEM((9, *codes.shape), jnp.int32),
            pltpu.SMEM((9, *codes.shape), jnp.int32),
            pltpu.VMEM(((fx + 2) * (fy + 2), kp + 1, b, 2 * b), bf),
            pltpu.VMEM((fx + 2, fy * b, win * b), bf),
            pltpu.VMEM(((fx + 2) * b, win * b), bf),
            pltpu.VMEM(((fx + 2) * b, win * b), bf),
            pltpu.VMEM((win * b, blocks * b), bf),
            pltpu.VMEM((fx * 3, fy * b, fy * b), bf),
            pltpu.VMEM((fx * b, (fx + 2) * b), bf),
            pltpu.VMEM((fx * b, (fx + 2) * b), bf),
            pltpu.VMEM((fx, fy * b, 5 * slab), f32),
            pltpu.VMEM((blocks * b, 5 * slab), bf),
            pltpu.VMEM((2, slab, 5 * slab), bf),
            pltpu.VMEM((2, slab, 5 * slab), bf),
            pltpu.VMEM((slab, 5 * slab), f32),
            pltpu.VMEM((n_row, rows, band), bf),
            pltpu.VMEM((n_row, rows, band), bf),
            dma((8,)), dma((8,)), dma((8,)), dma((8,)), dma, dma, dma,
            dma((2, n_row)), dma((2, n_row)), dma((n_row,)), dma((n_row,)),
        ],
        compiler_params=pltpu.CompilerParams(
            collective_id=0, has_side_effects=True, vmem_limit_bytes=50 * 1024 * 1024
        ),
    )(
        operator_tiles.reshape(-1, b, b), prolong_tiles.reshape(-1, b, b), ainv, codes, codes,
    )
    return out[None]


def solution(mesh):
    in_specs = (
        P("row", "col", None, None, None),
        P("row", "col", None),
        P("row", "col"),
        P("row", "col", None, None, None),
        P("row", "col", None),
    )
    out_specs = P("col", "row", None)
    return jax.shard_map(
        per_device, mesh=mesh, in_specs=in_specs, out_specs=out_specs, check_vma=False
    )
```

```python
import functools

import jax
import jax.numpy as jnp
from jax import lax
from jax.experimental import pallas as pl
from jax.experimental.pallas import tpu as pltpu
from jax.sharding import PartitionSpec as P

CB = 4
MESH = pl.DeviceIdType.MESH
STRIDE = 16


def kernel(
    dims, n_row, n_col, a_hbm, p_hbm, ainv_ref, live_ref, codes_smem, codes_ref, out_ref,
    a_ref, p_ref, pext, cext, csm, p2, wc, wl, wr, wt, ac, al, ar, acc, img,
    csend, crecv, own, zsend, zrecv,
    psend_sem, precv_sem, ksend_sem, krecv_sem, copy_sem, a_sem, p_sem,
    csend_sem, crecv_sem, zsend_sem, zrecv_sem,
):
    fx, fy, ka, kp, b = dims
    win = 3 * CB
    slab = CB * b
    rows = slab // n_row
    wide = 5 * slab
    me_r, me_c = lax.axis_index("row"), lax.axis_index("col")

    tiles_in = pltpu.make_async_copy(p_hbm, p_ref, p_sem)
    tiles_in.start()
    operator_in = pltpu.make_async_copy(a_hbm, a_ref, a_sem)
    operator_in.start()

    def device(dr, dc):
        return (lax.rem(me_r + dr + n_row, n_row), lax.rem(me_c + dc + n_col, n_col))

    around = [(i, j) for i in (-1, 0, 1) for j in (-1, 0, 1) if (i, j) != (0, 0)]
    partners = {(i % n_row, j % n_col) for i, j in around} | {(k, 0) for k in range(1, n_row)}
    barrier = pltpu.get_barrier_semaphore()
    for i, j in sorted(partners):
        pl.semaphore_signal(barrier, inc=1, device_id=device(i, j), device_id_type=MESH)

    def pack(n, carry):
        x, y = n // fy, n % fy
        for j in range(0, kp, 2):
            pair = [p_ref[n * kp + j], p_ref[n * kp + j + 1]]
            pext[x + 1, y + 1, :, j * b:(j + 2) * b] = jnp.concatenate(pair, axis=1)
        return carry

    tiles_in.wait()
    lax.fori_loop(0, fx * fy, pack, 0)
    pl.semaphore_wait(barrier, len(partners))

    halo = []
    for t, (i, j) in enumerate(around):
        xs = {-1: 1, 0: pl.ds(1, fx), 1: fx}[i]
        ys = {-1: 1, 0: pl.ds(1, fy), 1: fy}[j]
        xd = {-1: fx + 1, 0: pl.ds(1, fx), 1: 0}[i]
        yd = {-1: fy + 1, 0: pl.ds(1, fy), 1: 0}[j]
        numbers = pltpu.make_async_remote_copy(
            src_ref=codes_ref, dst_ref=cext.at[(1 - i) * 3 + 1 - j],
            send_sem=ksend_sem.at[t], recv_sem=krecv_sem.at[t],
            device_id=device(i, j), device_id_type=MESH,
        )
        tiles = pltpu.make_async_remote_copy(
            src_ref=pext.at[xs, ys], dst_ref=pext.at[xd, yd],
            send_sem=psend_sem.at[t], recv_sem=precv_sem.at[t],
            device_id=device(i, j), device_id_type=MESH,
        )
        halo += [numbers, tiles]
    for copy in halo:
        copy.start()

    lane = lax.broadcasted_iota(jnp.int32, (b, 2 * b), 1)
    lower = lane < b

    def spread(xe, ye, n, read, dst, at):
        e = xe * (fy + 2) + ye
        p2[e, kp] = jnp.zeros((b, 2 * b), p2.dtype)
        for j in range(0, kp, 2):
            pair = pext[xe, ye, :, j * b:(j + 2) * b]
            for h in range(2):
                tile = pair[:, h * b:(h + 1) * b]
                p2[e, j + h] = jnp.concatenate([tile, tile], axis=1)
        for w in range(0, win, 2):
            flat = n * STRIDE + w
            first, second = read(flat), read(flat + 1)
            dst(at, w * b, jnp.where(lower, p2[e, first], p2[e, second]))

    def to_centre(at, c, value):
        wc[at[0], pl.ds(at[1], b), c:c + 2 * b] = value

    def to_left(at, c, value):
        wl[pl.ds(at, b), c:c + 2 * b] = value

    def to_right(at, c, value):
        wr[pl.ds(at, b), c:c + 2 * b] = value

    def read_own(flat):
        return codes_smem[flat // 128, flat % 128]

    def read_near(slot):
        return lambda flat: csm[slot, flat // 128, flat % 128]

    def own_spread(n, carry):
        x, y = n // fy, n % fy
        spread(x + 1, y + 1, n, read_own, to_centre, (x + 1, pl.multiple_of(y * b, b)))
        return carry

    lax.fori_loop(0, fx * fy, own_spread, 0)

    def operator_tile(m, d):
        k = ainv_ref[m * 9 + d]
        tile = a_ref[m * ka + jnp.minimum(k, ka - 1)]
        used = jnp.full(tile.shape, k) < jnp.full(tile.shape, live_ref[m // fy, m % fy])
        return jnp.where(used, tile, jnp.zeros_like(tile))

    zero_tile = jnp.zeros((b, b), a_ref.dtype)
    operator_in.wait()

    def bands(x, carry):
        for dx in range(3):
            for y in range(fy):
                for yp in range(0, fy, 2):
                    pair = [
                        operator_tile(x * fy + y, dx * 3 + yy - y + 1) if abs(yy - y) < 2 else zero_tile
                        for yy in (yp, yp + 1)
                    ]
                    ac[x * 3 + dx, y * b:(y + 1) * b, yp * b:(yp + 2) * b] = jnp.concatenate(pair, axis=1)
        return carry

    lax.fori_loop(0, fx, bands, 0)
    for x in range(fx):
        for side, y, dy in ((al, 0, 0), (ar, fy - 1, 2)):
            for xe in range(0, fx + 2, 2):
                pair = [
                    operator_tile(x * fy + y, (xx - x) * 3 + dy) if 0 <= xx - x <= 2 else zero_tile
                    for xx in (xe, xe + 1)
                ]
                side[x * b:(x + 1) * b, xe * b:(xe + 2) * b] = jnp.concatenate(pair, axis=1)

    def own_transposed(x, carry):
        for c in range(3):
            wt[c * slab:(c + 1) * slab, pl.ds(pl.multiple_of(x * fy * b, fy * b), fy * b)] = (
                wc[x + 1, :, c * slab:(c + 1) * slab].T
            )
        return carry

    lax.fori_loop(0, fx, own_transposed, 0)

    for x in range(fx):
        acc[x, :, 0:slab] = jnp.zeros((fy * b, slab), jnp.float32)
        acc[x, :, 4 * slab:] = jnp.zeros((fy * b, slab), jnp.float32)
        total = None
        for dx in range(3):
            if 1 <= x + dx <= fx:
                term = jnp.dot(ac[x * 3 + dx], wc[x + dx], preferred_element_type=jnp.float32)
                total = term if total is None else total + term
        acc[x, :, slab:4 * slab] = total

    for copy in halo[::2]:
        copy.wait_recv()
    numbers_in = pltpu.make_async_copy(cext, csm, copy_sem)
    numbers_in.start()
    numbers_in.wait()

    def arrived(i, j):
        halo[2 * around.index((-i, -j)) + 1].wait_recv()

    def left_column(x, carry):
        at = pl.multiple_of((x + 1) * b, b)
        spread(x + 1, 0, x * fy + fy - 1, read_near(3), to_left, at)
        return carry

    def right_column(x, carry):
        at = pl.multiple_of((x + 1) * b, b)
        spread(x + 1, fy + 1, x * fy, read_near(5), to_right, at)
        return carry

    def top_row(y, carry):
        spread(0, y + 1, (fx - 1) * fy + y, read_near(1), to_centre, (0, pl.multiple_of(y * b, b)))
        return carry

    def bottom_row(y, carry):
        spread(fx + 1, y + 1, y, read_near(7), to_centre, (fx + 1, pl.multiple_of(y * b, b)))
        return carry

    arrived(0, -1)
    lax.fori_loop(0, fx, left_column, 0)
    arrived(0, 1)
    lax.fori_loop(0, fx, right_column, 0)
    arrived(-1, -1)
    spread(0, 0, fx * fy - 1, read_near(0), to_left, 0)
    arrived(1, -1)
    spread(fx + 1, 0, fy - 1, read_near(6), to_left, (fx + 1) * b)
    left = jnp.dot(al[...], wl[...], preferred_element_type=jnp.float32)
    for x in range(fx):
        acc[x, 0:b, 0:3 * slab] += left[x * b:(x + 1) * b]
    arrived(-1, 1)
    spread(0, fy + 1, (fx - 1) * fy, read_near(2), to_right, 0)
    arrived(1, 1)
    spread(fx + 1, fy + 1, 0, read_near(8), to_right, (fx + 1) * b)
    right = jnp.dot(ar[...], wr[...], preferred_element_type=jnp.float32)
    for x in range(fx):
        acc[x, (fy - 1) * b:, 2 * slab:] += right[x * b:(x + 1) * b]
    arrived(-1, 0)
    lax.fori_loop(0, fy, top_row, 0)
    acc[0, :, slab:4 * slab] += jnp.dot(ac[0], wc[0], preferred_element_type=jnp.float32)
    arrived(1, 0)
    lax.fori_loop(0, fy, bottom_row, 0)
    acc[fx - 1, :, slab:4 * slab] += jnp.dot(
        ac[(fx - 1) * 3 + 2], wc[fx + 1], preferred_element_type=jnp.float32
    )
    for x in range(fx):
        img[x * fy * b:(x + 1) * fy * b, :] = acc[x].astype(img.dtype)

    relayed = n_row == 4
    if relayed:
        far = jnp.where(2 * me_r < n_row, 3, 1)
        order = [2, far, n_row - far, 0]
    else:
        order = [*range(1, n_row), 0]
    across = []
    for side, part, step in ((0, 0, -1), (1, 2, 1)):
        for c in range(5):
            piece = jnp.dot(
                wt[part * slab:(part + 1) * slab, :], img[:, c * slab:(c + 1) * slab],
                preferred_element_type=jnp.float32,
            ).astype(csend.dtype)
            csend[side, :, c * slab:(c + 1) * slab] = piece
        for turn, k in enumerate(order):
            t = pl.multiple_of(lax.rem(me_r + k, n_row) * rows, rows)
            copy = pltpu.make_async_remote_copy(
                src_ref=csend.at[side, pl.ds(t, rows)], dst_ref=crecv.at[side, pl.ds(t, rows)],
                send_sem=csend_sem.at[side, turn], recv_sem=crecv_sem.at[side, turn],
                device_id=device(0, step), device_id_type=MESH,
            )
            copy.start()
            across.append((turn, copy))
    for c in range(5):
        own[:, c * slab:(c + 1) * slab] = jnp.dot(
            wt[slab:2 * slab, :], img[:, c * slab:(c + 1) * slab], preferred_element_type=jnp.float32
        )

    def combined(t):
        mine = own[pl.ds(t, rows), :]
        from_next = crecv[0, pl.ds(t, rows), :].astype(jnp.float32)
        from_prev = crecv[1, pl.ds(t, rows), :].astype(jnp.float32)
        parts = []
        for c in range(7):
            terms = [
                value[:, (c - shift) * slab:(c - shift + 1) * slab]
                for value, shift in ((mine, 1), (from_next, 2), (from_prev, 0))
                if 0 <= c - shift < 5
            ]
            parts.append(functools.reduce(jnp.add, terms))
        return parts

    inner = (me_r > 0) & (me_r < n_row - 1)
    down = []
    for turn, k in enumerate(order):
        last = turn == n_row - 2
        for other, copy in across:
            if other == turn:
                copy.wait_recv()
        t = pl.multiple_of(lax.rem(me_r + k, n_row) * rows, rows)
        if relayed and last:
            @pl.when(inner)
            def _():
                down[0].wait_recv()

        for c, value in enumerate(combined(t)):
            at = slice(c * slab, (c + 1) * slab)
            if turn == n_row - 1:
                out_ref[:, at] = value
                continue
            zsend[turn, :, at] = value.astype(zsend.dtype)
            if relayed and last:
                @pl.when(inner)
                def _(value=value, at=at):
                    zsend[turn, :, at] = (value + zrecv[2, :, at].astype(jnp.float32)).astype(zsend.dtype)
        if turn == n_row - 1:
            continue
        steps = k
        if relayed and turn == 0:
            steps = jnp.where(inner, 2, jnp.where(me_r == 0, 1, n_row - 1))
        copy = pltpu.make_async_remote_copy(
            src_ref=zsend.at[turn], dst_ref=zrecv.at[k],
            send_sem=zsend_sem.at[turn], recv_sem=zrecv_sem.at[k],
            device_id=device(steps, 0), device_id_type=MESH,
        )
        copy.start()
        down.append(copy)

    def take(k):
        out_ref[...] += zrecv[k].astype(jnp.float32)

    if relayed:
        for k, copy in enumerate(down):
            if k == 0:
                @pl.when(jnp.logical_not(inner))
                def _():
                    down[0].wait_recv()
                    take(2)
            else:
                copy.wait_recv()
                take(order[k])
    else:
        for turn, copy in enumerate(down):
            copy.wait_recv()
            take(order[turn])
    for copy in halo:
        copy.wait_send()
    for copy in [copy for _, copy in across] + down:
        copy.wait_send()


def per_device(operator_tiles, neighbour_codes, live_slots, prolong_tiles, coarse_blocks):
    fx, fy, ka = neighbour_codes.shape
    kp = prolong_tiles.shape[2]
    b = operator_tiles.shape[-1]
    n_row, n_col = lax.axis_size("row"), lax.axis_size("col")
    slab_index = lax.axis_index("col")
    win = 3 * CB
    slab = CB * b
    rows = slab // n_row
    band = 7 * slab
    blocks = fx * fy
    slots = jnp.arange(ka, dtype=jnp.int32)[:, None]
    match = neighbour_codes[..., None] == jnp.arange(9, dtype=jnp.int32)
    ainv = jnp.min(jnp.where(match, slots, ka), axis=2).reshape(-1)
    place = jnp.mod(coarse_blocks // CB - slab_index + 1, n_col) * CB + coarse_blocks % CB
    tiles = jnp.arange(kp, dtype=jnp.int32)[:, None]
    hit = place[..., None] == jnp.arange(STRIDE, dtype=jnp.int32)
    pinv = jnp.min(jnp.where(hit, tiles, kp), axis=2).reshape(-1, 128)
    codes = jnp.pad(pinv, ((0, -pinv.shape[0] % 8), (0, 0)))
    bf, f32 = jnp.bfloat16, jnp.float32
    dma = pltpu.SemaphoreType.DMA
    vmem = pl.BlockSpec(memory_space=pltpu.VMEM)
    hbm = pl.BlockSpec(memory_space=pltpu.HBM)
    smem = pl.BlockSpec(memory_space=pltpu.SMEM)
    out = pl.pallas_call(
        functools.partial(kernel, (fx, fy, ka, kp, b), n_row, n_col),
        out_shape=jax.ShapeDtypeStruct((rows, band), f32),
        in_specs=[hbm, hbm, smem, smem, smem, vmem],
        out_specs=vmem,
        scratch_shapes=[
            pltpu.VMEM((blocks * ka, b, b), bf),
            pltpu.VMEM((blocks * kp, b, b), bf),
            pltpu.VMEM((fx + 2, fy + 2, b, kp * b), bf),
            pltpu.VMEM((9, *codes.shape), jnp.int32),
            pltpu.SMEM((9, *codes.shape), jnp.int32),
            pltpu.VMEM(((fx + 2) * (fy + 2), kp + 1, b, 2 * b), bf),
            pltpu.VMEM((fx + 2, fy * b, win * b), bf),
            pltpu.VMEM(((fx + 2) * b, win * b), bf),
            pltpu.VMEM(((fx + 2) * b, win * b), bf),
            pltpu.VMEM((win * b, blocks * b), bf),
            pltpu.VMEM((fx * 3, fy * b, fy * b), bf),
            pltpu.VMEM((fx * b, (fx + 2) * b), bf),
            pltpu.VMEM((fx * b, (fx + 2) * b), bf),
            pltpu.VMEM((fx, fy * b, 5 * slab), f32),
            pltpu.VMEM((blocks * b, 5 * slab), bf),
            pltpu.VMEM((2, slab, 5 * slab), bf),
            pltpu.VMEM((2, slab, 5 * slab), bf),
            pltpu.VMEM((slab, 5 * slab), f32),
            pltpu.VMEM((n_row, rows, band), bf),
            pltpu.VMEM((n_row, rows, band), bf),
            dma((8,)), dma((8,)), dma((8,)), dma((8,)), dma, dma, dma,
            dma((2, n_row)), dma((2, n_row)), dma((n_row,)), dma((n_row,)),
        ],
        compiler_params=pltpu.CompilerParams(
            collective_id=0, has_side_effects=True, vmem_limit_bytes=50 * 1024 * 1024
        ),
    )(
        operator_tiles.reshape(-1, b, b), prolong_tiles.reshape(-1, b, b), ainv, live_slots, codes, codes,
    )
    return out[None]


def solution(mesh):
    in_specs = (
        P("row", "col", None, None, None),
        P("row", "col", None),
        P("row", "col"),
        P("row", "col", None, None, None),
        P("row", "col", None),
    )
    out_specs = P("col", "row", None)
    return jax.shard_map(
        per_device, mesh=mesh, in_specs=in_specs, out_specs=out_specs, check_vma=False
    )
```

```python
import functools

import jax
import jax.numpy as jnp
from jax import lax
from jax.experimental import pallas as pl
from jax.experimental.pallas import tpu as pltpu
from jax.sharding import PartitionSpec as P

CB = 4
MESH = pl.DeviceIdType.MESH
STRIDE = 16


def kernel(
    dims, n_row, n_col, a_hbm, p_hbm, ainv_ref, codes_smem, codes_ref, out_ref,
    a_ref, p_ref, pext, cext, csm, p2, wc, wl, wr, wt, ac, al, ar, acc, img,
    csend, crecv, own, zsend, zrecv,
    psend_sem, precv_sem, ksend_sem, krecv_sem, copy_sem, a_sem, p_sem,
    csend_sem, crecv_sem, zsend_sem, zrecv_sem,
):
    fx, fy, ka, kp, b = dims
    win = 3 * CB
    slab = CB * b
    rows = slab // n_row
    wide = 5 * slab
    me_r, me_c = lax.axis_index("row"), lax.axis_index("col")

    tiles_in = pltpu.make_async_copy(p_hbm, p_ref, p_sem)
    tiles_in.start()
    operator_in = pltpu.make_async_copy(a_hbm, a_ref, a_sem)
    operator_in.start()

    def device(dr, dc):
        return (lax.rem(me_r + dr + n_row, n_row), lax.rem(me_c + dc + n_col, n_col))

    around = [(i, j) for i in (-1, 0, 1) for j in (-1, 0, 1) if (i, j) != (0, 0)]
    partners = {(i % n_row, j % n_col) for i, j in around} | {(k, 0) for k in range(1, n_row)}
    barrier = pltpu.get_barrier_semaphore()
    for i, j in sorted(partners):
        pl.semaphore_signal(barrier, inc=1, device_id=device(i, j), device_id_type=MESH)

    def pack(n, carry):
        x, y = n // fy, n % fy
        for j in range(0, kp, 2):
            pair = [p_ref[n * kp + j], p_ref[n * kp + j + 1]]
            pext[x + 1, y + 1, :, j * b:(j + 2) * b] = jnp.concatenate(pair, axis=1)
        return carry

    tiles_in.wait()
    lax.fori_loop(0, fx * fy, pack, 0)
    pl.semaphore_wait(barrier, len(partners))

    halo = []
    for t, (i, j) in enumerate(around):
        xs = {-1: 1, 0: pl.ds(1, fx), 1: fx}[i]
        ys = {-1: 1, 0: pl.ds(1, fy), 1: fy}[j]
        xd = {-1: fx + 1, 0: pl.ds(1, fx), 1: 0}[i]
        yd = {-1: fy + 1, 0: pl.ds(1, fy), 1: 0}[j]
        numbers = pltpu.make_async_remote_copy(
            src_ref=codes_ref, dst_ref=cext.at[(1 - i) * 3 + 1 - j],
            send_sem=ksend_sem.at[t], recv_sem=krecv_sem.at[t],
            device_id=device(i, j), device_id_type=MESH,
        )
        tiles = pltpu.make_async_remote_copy(
            src_ref=pext.at[xs, ys], dst_ref=pext.at[xd, yd],
            send_sem=psend_sem.at[t], recv_sem=precv_sem.at[t],
            device_id=device(i, j), device_id_type=MESH,
        )
        halo += [numbers, tiles]
    for copy in halo[::2]:
        copy.start()
    for t in sorted(range(len(around)), key=lambda t: (around[t][0] == 0, around[t][1] != 0)):
        halo[2 * t + 1].start()

    lane = lax.broadcasted_iota(jnp.int32, (b, 2 * b), 1)
    lower = lane < b

    def spread(xe, ye, n, read, dst, at):
        e = xe * (fy + 2) + ye
        p2[e, kp] = jnp.zeros((b, 2 * b), p2.dtype)
        for j in range(0, kp, 2):
            pair = pext[xe, ye, :, j * b:(j + 2) * b]
            for h in range(2):
                tile = pair[:, h * b:(h + 1) * b]
                p2[e, j + h] = jnp.concatenate([tile, tile], axis=1)
        for w in range(0, win, 2):
            flat = n * STRIDE + w
            first, second = read(flat), read(flat + 1)
            dst(at, w * b, jnp.where(lower, p2[e, first], p2[e, second]))

    def to_centre(at, c, value):
        wc[at[0], pl.ds(at[1], b), c:c + 2 * b] = value

    def to_left(at, c, value):
        wl[pl.ds(at, b), c:c + 2 * b] = value

    def to_right(at, c, value):
        wr[pl.ds(at, b), c:c + 2 * b] = value

    def read_own(flat):
        return codes_smem[flat // 128, flat % 128]

    def read_near(slot):
        return lambda flat: csm[slot, flat // 128, flat % 128]

    def own_spread(n, carry):
        x, y = n // fy, n % fy
        spread(x + 1, y + 1, n, read_own, to_centre, (x + 1, pl.multiple_of(y * b, b)))
        return carry

    lax.fori_loop(0, fx * fy, own_spread, 0)

    def operator_tile(m, d):
        k = ainv_ref[m * 9 + d]
        tile = a_ref[m * ka + jnp.minimum(k, ka - 1)]
        return jnp.where(jnp.full(tile.shape, k) < ka, tile, jnp.zeros_like(tile))

    zero_tile = jnp.zeros((b, b), a_ref.dtype)
    operator_in.wait()

    def bands(x, carry):
        for dx in range(3):
            for y in range(fy):
                for yp in range(0, fy, 2):
                    pair = [
                        operator_tile(x * fy + y, dx * 3 + yy - y + 1) if abs(yy - y) < 2 else zero_tile
                        for yy in (yp, yp + 1)
                    ]
                    ac[x * 3 + dx, y * b:(y + 1) * b, yp * b:(yp + 2) * b] = jnp.concatenate(pair, axis=1)
        return carry

    lax.fori_loop(0, fx, bands, 0)
    for x in range(fx):
        for side, y, dy in ((al, 0, 0), (ar, fy - 1, 2)):
            for xe in range(0, fx + 2, 2):
                pair = [
                    operator_tile(x * fy + y, (xx - x) * 3 + dy) if 0 <= xx - x <= 2 else zero_tile
                    for xx in (xe, xe + 1)
                ]
                side[x * b:(x + 1) * b, xe * b:(xe + 2) * b] = jnp.concatenate(pair, axis=1)

    def own_transposed(x, carry):
        for c in range(3):
            wt[c * slab:(c + 1) * slab, pl.ds(pl.multiple_of(x * fy * b, fy * b), fy * b)] = (
                wc[x + 1, :, c * slab:(c + 1) * slab].T
            )
        return carry

    lax.fori_loop(0, fx, own_transposed, 0)

    for x in range(fx):
        acc[x, :, 0:slab] = jnp.zeros((fy * b, slab), jnp.float32)
        acc[x, :, 4 * slab:] = jnp.zeros((fy * b, slab), jnp.float32)
        total = None
        for dx in range(3):
            if 1 <= x + dx <= fx:
                term = jnp.dot(ac[x * 3 + dx], wc[x + dx], preferred_element_type=jnp.float32)
                total = term if total is None else total + term
        acc[x, :, slab:4 * slab] = total

    for copy in halo:
        copy.wait_recv()
    numbers_in = pltpu.make_async_copy(cext, csm, copy_sem)
    numbers_in.start()
    numbers_in.wait()

    def edge_rows(y, carry):
        at = pl.multiple_of(y * b, b)
        spread(0, y + 1, (fx - 1) * fy + y, read_near(1), to_centre, (0, at))
        spread(fx + 1, y + 1, y, read_near(7), to_centre, (fx + 1, at))
        return carry

    lax.fori_loop(0, fy, edge_rows, 0)

    def edge_columns(x, carry):
        at = pl.multiple_of((x + 1) * b, b)
        spread(x + 1, 0, x * fy + fy - 1, read_near(3), to_left, at)
        spread(x + 1, fy + 1, x * fy, read_near(5), to_right, at)
        return carry

    lax.fori_loop(0, fx, edge_columns, 0)
    spread(0, 0, fx * fy - 1, read_near(0), to_left, 0)
    spread(0, fy + 1, (fx - 1) * fy, read_near(2), to_right, 0)
    spread(fx + 1, 0, fy - 1, read_near(6), to_left, (fx + 1) * b)
    spread(fx + 1, fy + 1, 0, read_near(8), to_right, (fx + 1) * b)

    acc[0, :, slab:4 * slab] += jnp.dot(ac[0], wc[0], preferred_element_type=jnp.float32)
    acc[fx - 1, :, slab:4 * slab] += jnp.dot(
        ac[(fx - 1) * 3 + 2], wc[fx + 1], preferred_element_type=jnp.float32
    )
    left = jnp.dot(al[...], wl[...], preferred_element_type=jnp.float32)
    for x in range(fx):
        acc[x, 0:b, 0:3 * slab] += left[x * b:(x + 1) * b]
    right = jnp.dot(ar[...], wr[...], preferred_element_type=jnp.float32)
    for x in range(fx):
        acc[x, (fy - 1) * b:, 2 * slab:] += right[x * b:(x + 1) * b]
    for x in range(fx):
        img[x * fy * b:(x + 1) * fy * b, :] = acc[x].astype(img.dtype)

    relayed = n_row == 4
    if relayed:
        far = jnp.where(2 * me_r < n_row, 3, 1)
        order = [2, far, n_row - far, 0]
    else:
        order = [*range(1, n_row), 0]
    across = []
    for side, part, step in ((0, 0, -1), (1, 2, 1)):
        for c in range(5):
            piece = jnp.dot(
                wt[part * slab:(part + 1) * slab, :], img[:, c * slab:(c + 1) * slab],
                preferred_element_type=jnp.float32,
            ).astype(csend.dtype)
            csend[side, :, c * slab:(c + 1) * slab] = piece
        for turn, k in enumerate(order):
            t = pl.multiple_of(lax.rem(me_r + k, n_row) * rows, rows)
            copy = pltpu.make_async_remote_copy(
                src_ref=csend.at[side, pl.ds(t, rows)], dst_ref=crecv.at[side, pl.ds(t, rows)],
                send_sem=csend_sem.at[side, turn], recv_sem=crecv_sem.at[side, turn],
                device_id=device(0, step), device_id_type=MESH,
            )
            copy.start()
            across.append((turn, copy))
    for c in range(5):
        own[:, c * slab:(c + 1) * slab] = jnp.dot(
            wt[slab:2 * slab, :], img[:, c * slab:(c + 1) * slab], preferred_element_type=jnp.float32
        )

    def combined(t):
        mine = own[pl.ds(t, rows), :]
        from_next = crecv[0, pl.ds(t, rows), :].astype(jnp.float32)
        from_prev = crecv[1, pl.ds(t, rows), :].astype(jnp.float32)
        parts = []
        for c in range(7):
            terms = [
                value[:, (c - shift) * slab:(c - shift + 1) * slab]
                for value, shift in ((mine, 1), (from_next, 2), (from_prev, 0))
                if 0 <= c - shift < 5
            ]
            parts.append(functools.reduce(jnp.add, terms))
        return parts

    inner = (me_r > 0) & (me_r < n_row - 1)
    down = []
    for turn, k in enumerate(order):
        last = turn == n_row - 2
        for other, copy in across:
            if other == turn:
                copy.wait_recv()
        t = pl.multiple_of(lax.rem(me_r + k, n_row) * rows, rows)
        if relayed and last:
            @pl.when(inner)
            def _():
                down[0].wait_recv()

        for c, value in enumerate(combined(t)):
            at = slice(c * slab, (c + 1) * slab)
            if turn == n_row - 1:
                out_ref[:, at] = value
                continue
            zsend[turn, :, at] = value.astype(zsend.dtype)
            if relayed and last:
                @pl.when(inner)
                def _(value=value, at=at):
                    zsend[turn, :, at] = (value + zrecv[2, :, at].astype(jnp.float32)).astype(zsend.dtype)
        if turn == n_row - 1:
            continue
        steps = k
        if relayed and turn == 0:
            steps = jnp.where(inner, 2, jnp.where(me_r == 0, 1, n_row - 1))
        copy = pltpu.make_async_remote_copy(
            src_ref=zsend.at[turn], dst_ref=zrecv.at[k],
            send_sem=zsend_sem.at[turn], recv_sem=zrecv_sem.at[k],
            device_id=device(steps, 0), device_id_type=MESH,
        )
        copy.start()
        down.append(copy)

    def take(k):
        out_ref[...] += zrecv[k].astype(jnp.float32)

    if relayed:
        for k, copy in enumerate(down):
            if k == 0:
                @pl.when(jnp.logical_not(inner))
                def _():
                    down[0].wait_recv()
                    take(2)
            else:
                copy.wait_recv()
                take(order[k])
    else:
        for turn, copy in enumerate(down):
            copy.wait_recv()
            take(order[turn])
    for copy in halo:
        copy.wait_send()
    for copy in [copy for _, copy in across] + down:
        copy.wait_send()


def per_device(operator_tiles, neighbour_codes, live_slots, prolong_tiles, coarse_blocks):
    fx, fy, ka = neighbour_codes.shape
    kp = prolong_tiles.shape[2]
    b = operator_tiles.shape[-1]
    n_row, n_col = lax.axis_size("row"), lax.axis_size("col")
    slab_index = lax.axis_index("col")
    win = 3 * CB
    slab = CB * b
    rows = slab // n_row
    band = 7 * slab
    blocks = fx * fy
    slots = jnp.arange(ka, dtype=jnp.int32)[:, None]
    match = (neighbour_codes[..., None] == jnp.arange(9, dtype=jnp.int32)) & (slots < live_slots[..., None, None])
    ainv = jnp.min(jnp.where(match, slots, ka), axis=2).reshape(-1)
    place = jnp.mod(coarse_blocks // CB - slab_index + 1, n_col) * CB + coarse_blocks % CB
    tiles = jnp.arange(kp, dtype=jnp.int32)[:, None]
    hit = place[..., None] == jnp.arange(STRIDE, dtype=jnp.int32)
    pinv = jnp.min(jnp.where(hit, tiles, kp), axis=2).reshape(-1, 128)
    codes = jnp.pad(pinv, ((0, -pinv.shape[0] % 8), (0, 0)))
    bf, f32 = jnp.bfloat16, jnp.float32
    dma = pltpu.SemaphoreType.DMA
    vmem = pl.BlockSpec(memory_space=pltpu.VMEM)
    hbm = pl.BlockSpec(memory_space=pltpu.HBM)
    smem = pl.BlockSpec(memory_space=pltpu.SMEM)
    out = pl.pallas_call(
        functools.partial(kernel, (fx, fy, ka, kp, b), n_row, n_col),
        out_shape=jax.ShapeDtypeStruct((rows, band), f32),
        in_specs=[hbm, hbm, smem, smem, vmem],
        out_specs=vmem,
        scratch_shapes=[
            pltpu.VMEM((blocks * ka, b, b), bf),
            pltpu.VMEM((blocks * kp, b, b), bf),
            pltpu.VMEM((fx + 2, fy + 2, b, kp * b), bf),
            pltpu.VMEM((9, *codes.shape), jnp.int32),
            pltpu.SMEM((9, *codes.shape), jnp.int32),
            pltpu.VMEM(((fx + 2) * (fy + 2), kp + 1, b, 2 * b), bf),
            pltpu.VMEM((fx + 2, fy * b, win * b), bf),
            pltpu.VMEM(((fx + 2) * b, win * b), bf),
            pltpu.VMEM(((fx + 2) * b, win * b), bf),
            pltpu.VMEM((win * b, blocks * b), bf),
            pltpu.VMEM((fx * 3, fy * b, fy * b), bf),
            pltpu.VMEM((fx * b, (fx + 2) * b), bf),
            pltpu.VMEM((fx * b, (fx + 2) * b), bf),
            pltpu.VMEM((fx, fy * b, 5 * slab), f32),
            pltpu.VMEM((blocks * b, 5 * slab), bf),
            pltpu.VMEM((2, slab, 5 * slab), bf),
            pltpu.VMEM((2, slab, 5 * slab), bf),
            pltpu.VMEM((slab, 5 * slab), f32),
            pltpu.VMEM((n_row, rows, band), bf),
            pltpu.VMEM((n_row, rows, band), bf),
            dma((8,)), dma((8,)), dma((8,)), dma((8,)), dma, dma, dma,
            dma((2, n_row)), dma((2, n_row)), dma((n_row,)), dma((n_row,)),
        ],
        compiler_params=pltpu.CompilerParams(
            collective_id=0, has_side_effects=True, vmem_limit_bytes=60 * 1024 * 1024
        ),
    )(
        operator_tiles.reshape(-1, b, b), prolong_tiles.reshape(-1, b, b), ainv, codes, codes,
    )
    return out[None]


def solution(mesh):
    in_specs = (
        P("row", "col", None, None, None),
        P("row", "col", None),
        P("row", "col"),
        P("row", "col", None, None, None),
        P("row", "col", None),
    )
    out_specs = P("col", "row", None)
    return jax.shard_map(
        per_device, mesh=mesh, in_specs=in_specs, out_specs=out_specs, check_vma=False
    )
```
